32 devices in a mesh: row: 16 (over z, x, core), col: 2 (over y).
Axes of the slice: x: 2, y: 2, z: 4, core: 2. Of those that a mesh axis runs over, the one named last changes fastest.
Arguments:
- gbar: float32 [8192, 8192], P('row', 'col'), may hold values from -9 to 9, as said below
- panels: float32 [8192, 1024], P('row'), may hold values from -0.0625 to 0.0625
- panel_cot: float32 [8192, 1024], P('row'), may hold values from -6 to 6
- inverses: float32 [2, 512, 512], replicated, may hold values from -1 to 2, as said below
Outputs:
- adjoint: float32 [8192, 1024], P('row')
- diag_adjoint: float32 [2, 512, 512], P(None, 'row')
The draws below stay inside these ranges and needn't reach their ends.
Inputs may be any that keep to these rules, and one draw needn't show every extreme that they name: G, formed from gbar as in the reference program, is symmetric. Each inverses[i] is lower triangular with diagonal entries between 1 and 2.
All inputs are finite; a program needn't handle non-finite values.
Results may differ from the reference program's by a relative error of at most 0.000071.
Values sent between devices are 32-bit elements; how exact they have to be, the bound alone decides.
A program may use at most 128 MiB of HBM per device.

```python
import jax
import jax.numpy as jnp
from jax import lax

B = 512
NT = 16
KC = 8
M = 8192
N_COL = 2


def draw_gbar(key, part):
    order_total = NT * B
    raw = jnp.clip(jax.random.normal(key, (order_total, order_total), jnp.float32), -6.0, 6.0)
    symmetric = (raw + raw.T) * 0.70710678
    stored = symmetric.reshape(order_total, KC, NT // KC, B).transpose(0, 2, 1, 3).reshape(order_total, order_total)
    return stored


def draw_inverses(key, part):
    diag_key = jax.random.fold_in(key, 11)
    off_key = jax.random.fold_in(key, 23)
    diagonal = jax.random.uniform(diag_key, (2, B), jnp.float32, 1.0, 2.0)
    below = jnp.clip(jax.random.normal(off_key, (2, B, B), jnp.float32), -4.0, 4.0) * (0.6 / B ** 0.5)
    rows_idx = jnp.arange(B)[:, None]
    cols_idx = jnp.arange(B)[None, :]
    lower = jnp.where(rows_idx > cols_idx, 1.0, 0.0).astype(jnp.float32)
    eye_mat = jnp.where(rows_idx == cols_idx, 1.0, 0.0).astype(jnp.float32)
    return below * lower[None] + diagonal[:, :, None] * eye_mat[None]


def levels(own_key, shape, pieces, low, top_value):
    gain, own = 1.0, jax.random.fold_in(own_key, 6)
    for axis_at, blocks in pieces:
        steps = jnp.exp(jax.random.uniform(jax.random.fold_in(own, axis_at), (blocks,), jnp.float32, low / len(pieces), top_value / len(pieces)))
        gain = gain * jnp.repeat(steps, shape[axis_at] // blocks).reshape([-1 if axis == axis_at else 1 for axis in range(len(shape))])
    return gain


def normal_values(own_key, shape, deviation, limit, shards=(), held_as=jnp.bfloat16):
    result = deviation * jax.random.normal(own_key, shape, jnp.float32)
    if shards:
        result = result * levels(own_key, shape, shards, -0.22, 0.18)
    return jnp.clip(result, -limit, limit).astype(held_as)


def setup_inputs(seed: int = 0) -> dict:
    seeds = jax.random.split(jax.random.key(seed), 5)
    gbar = draw_gbar(jax.random.fold_in(seeds[4], 71), 0)
    panels = normal_values(seeds[1], (M, 2 * B), M ** -0.5, 0.0625, ((0, 16),), jnp.float32)
    panel_cot = normal_values(seeds[2], (M, 2 * B), 1.0, 6.0, ((0, 16),), jnp.float32)
    inverses = draw_inverses(jax.random.fold_in(seeds[4], 71), 0)
    return dict(gbar=gbar, panels=panels, panel_cot=panel_cot, inverses=inverses)


def reference(gbar, panels, panel_cot, inverses):
    width = inverses.shape[-1]
    order_total = panels.shape[0]
    exact_mode = lax.Precision.HIGHEST
    reordered = panels.reshape(KC, N_COL, width, 2 * width).transpose(1, 0, 2, 3).reshape(order_total, 2 * width)
    coupled = jnp.dot(gbar, reordered, precision=exact_mode, preferred_element_type=jnp.float32)
    combined = panel_cot - 2.0 * coupled
    first_adj = jnp.dot(combined[:, :width], inverses[0], precision=exact_mode, preferred_element_type=jnp.float32)
    second_adj = jnp.dot(combined[:, width:], inverses[1], precision=exact_mode, preferred_element_type=jnp.float32)
    adjoint = jnp.concatenate([first_adj, second_adj], axis=1)
    first_diag = -jnp.dot(first_adj.T, panels[:, :width], precision=exact_mode, preferred_element_type=jnp.float32)
    second_diag = -jnp.dot(second_adj.T, panels[:, width:], precision=exact_mode, preferred_element_type=jnp.float32)
    return adjoint, jnp.stack([first_diag, second_diag])
```

```python
import jax
import jax.numpy as jnp
from jax import lax
from jax.experimental import pallas as pl
from jax.experimental.pallas import tpu as pltpu
from jax.sharding import PartitionSpec as P

MESH = pl.DeviceIdType.MESH
SUBS = 2


def halves(value):
    high = value.astype(jnp.bfloat16)
    low = (value - high.astype(jnp.float32)).astype(jnp.bfloat16)
    return high, low


def product(left, right):
    (left_high, left_low), (right_high, right_low) = left, right

    def one(a, b):
        return jnp.dot(a, b, preferred_element_type=jnp.float32)

    return one(left_high, right_low) + one(left_low, right_high) + one(left_high, right_high)


def ring_kernel(
    chips, gbar, panels, cot, inverses,
    adjoint, diag,
    g_v, p_v, cot_v, inv_v, p_high, p_low, terms, other, arrived, final, adj_v, diag_v,
    load_sems, out_sems, pair_send, pair_recv, ring_send, ring_recv, end_send, end_recv,
):
    width = inverses.shape[-1]
    lane = width // 4
    piece = lane // SUBS
    row = lax.axis_index("row")
    col = lax.axis_index("col")
    chip = row // 2
    core = row % 2
    mate = 1 - core
    half = chips // 2

    def place_of(chip_id):
        return jnp.where(chip_id % 2 == 0, chip_id // 2, chips - 1 - chip_id // 2)

    def chip_at(place):
        return jnp.where(place < half, 2 * place, 2 * (chips - 1 - place) + 1)

    place = place_of(chip)
    right = chip_at((place + 1) % chips)
    left = chip_at((place + chips - 1) % chips)

    def tile_at(way, step):
        ahead = jnp.where(way == 0, place + 2 * chips - 1 - step, place + 1 + step)
        return chip_at(ahead % chips)

    def load_g(tile):
        start = pl.multiple_of(tile * width, width)
        return pltpu.make_async_copy(gbar.at[:, pl.ds(start, width)], g_v.at[tile], load_sems.at[tile])

    load_p = pltpu.make_async_copy(panels, p_v, load_sems.at[chips])
    load_cot = pltpu.make_async_copy(cot, cot_v, load_sems.at[chips + 1])
    load_inv = pltpu.make_async_copy(inverses, inv_v, load_sems.at[chips + 2])
    load_p.start()
    for hop in (1, 2, 3):
        load_g(chip_at((place + chips - hop) % chips)).start()
        load_g(chip_at((place + hop) % chips)).start()
    load_g(chip_at((place + half) % chips)).start()
    load_g(chip).start()
    load_cot.start()
    load_inv.start()

    barrier = pltpu.get_barrier_semaphore()
    friends = [
        (2 * right + core, col),
        (2 * left + core, col),
        (2 * chip + mate, col),
        (2 * chip + core, 1 - col),
        (2 * chip + mate, 1 - col),
    ]
    for friend in friends:
        pl.semaphore_signal(barrier, inc=1, device_id=friend, device_id_type=MESH)

    load_p.wait()
    for block in range(4):
        rows = slice(block * width // 2, (block + 1) * width // 2)
        high, low = halves(p_v[:, rows].T)
        p_high[rows, :] = high
        p_low[rows, :] = low

    def pair_copy(panel, way, step):
        return pltpu.make_async_remote_copy(
            terms.at[panel, way, step, mate],
            other.at[panel, way, step],
            pair_send.at[panel, way, step],
            pair_recv.at[panel, way, step],
            device_id=(2 * chip + mate, col),
            device_id_type=MESH,
        )

    def ring_copy(panel, way, step, sub):
        target = jnp.where(way == 0, right, left)
        rows = pl.ds(sub * piece, piece)
        return pltpu.make_async_remote_copy(
            terms.at[panel, way, step, core, rows],
            arrived.at[panel, way, step, rows],
            ring_send.at[panel, way, step, sub],
            ring_recv.at[panel, way, step, sub],
            device_id=(2 * target + core, col),
            device_id_type=MESH,
        )

    def end_copy(panel, way, plane, source_core):
        return pltpu.make_async_remote_copy(
            terms.at[panel, way, chips - 1, source_core],
            final.at[panel, way, source_core],
            end_send.at[panel, way, plane],
            end_recv.at[panel, way, source_core],
            device_id=(2 * chip + col, jnp.where(plane == 0, col, 1 - col)),
            device_id_type=MESH,
        )

    def end_local(panel, way, source_core):
        return pltpu.make_async_copy(
            terms.at[panel, way, chips - 1, source_core],
            final.at[panel, way, source_core],
            end_recv.at[panel, way, source_core],
        )

    def make_terms(count):
        panel, step = count // chips, count % chips
        for way in (0, 1):
            tile = tile_at(way, step)

            @pl.when((panel == 0) & (step < half if way == 0 else step < half - 1))
            def _():
                load_g(tile).wait()

            @pl.when((panel == 0) & (step == chips - 1) & (way == 0))
            def _():
                load_g(tile).wait()

            rows = pl.ds(pl.multiple_of(panel * width + way * (width // 2), width // 2), width // 2)
            value = product((p_high[rows, :], p_low[rows, :]), halves(g_v[tile]))
            terms[panel, way, step, 0] = value[:lane]
            terms[panel, way, step, 1] = value[lane:]
            pair_copy(panel, way, step).start()

    def ring_step(count):
        panel, step = count // chips, count % chips
        for way in (0, 1):
            pair_copy(panel, way, step).wait_recv()
        for sub in range(SUBS):
            rows = pl.ds(sub * piece, piece)
            for way in (0, 1):
                @pl.when(step > 0)
                def _():
                    ring_copy(panel, way, step - 1, sub).wait_recv()
                    terms[panel, way, step, core, rows] = (
                        terms[panel, way, step, core, rows]
                        + other[panel, way, step, rows]
                        + arrived[panel, way, step - 1, rows]
                    )

                @pl.when(step == 0)
                def _():
                    terms[panel, way, step, core, rows] = (
                        terms[panel, way, step, core, rows] + other[panel, way, step, rows]
                    )

                @pl.when(step < chips - 1)
                def _():
                    ring_copy(panel, way, step, sub).start()

        @pl.when(step == chips - 1)
        def _():
            for way in (0, 1):
                end_copy(panel, way, 1, core).start()

                @pl.when(core == col)
                def _():
                    end_local(panel, way, core).start()

                @pl.when(core != col)
                def _():
                    end_copy(panel, way, 0, core).start()

    def finish(panel):
        for way in (0, 1):
            for source in (0, 1):
                end_local(panel, way, source).wait()
        columns = slice(panel * width, (panel + 1) * width)
        coupled = final[panel].reshape(width, width)
        combined = cot_v[:, columns].T - 2.0 * coupled
        turned = product(halves(inv_v[panel].T), halves(combined))
        adj_v[:, columns] = turned.T
        own = (p_v[:, columns])
        diag_v[panel] = -product(halves(turned), halves(own))
        pltpu.make_async_copy(adj_v.at[:, columns], adjoint.at[:, columns], out_sems.at[0, panel]).start()
        pltpu.make_async_copy(diag_v.at[panel], diag.at[panel], out_sems.at[1, panel]).start()

    pl.semaphore_wait(barrier, len(friends))
    make_terms(jnp.int32(0))
    load_cot.wait()
    load_inv.wait()

    def body(count, carry):
        @pl.when(count < 2 * chips - 1)
        def _():
            make_terms(count + 1)

        ring_step(count)

        @pl.when(count == chips + 2)
        def _():
            finish(0)

        return carry

    lax.fori_loop(0, 2 * chips, body, 0)
    finish(1)

    def drain(count, carry):
        panel, step = count // chips, count % chips
        for way in (0, 1):
            pair_copy(panel, way, step).wait_send()

            @pl.when(step < chips - 1)
            def _():
                for sub in range(SUBS):
                    ring_copy(panel, way, step, sub).wait_send()

        return carry

    lax.fori_loop(0, 2 * chips, drain, 0)
    for panel in (0, 1):
        columns = slice(panel * width, (panel + 1) * width)
        for way in (0, 1):
            end_copy(panel, way, 1, core).wait_send()

            @pl.when(core != col)
            def _():
                end_copy(panel, way, 0, core).wait_send()

        pltpu.make_async_copy(adj_v.at[:, columns], adjoint.at[:, columns], out_sems.at[0, panel]).wait()
        pltpu.make_async_copy(diag_v.at[panel], diag.at[panel], out_sems.at[1, panel]).wait()


def ring_device(gbar, panels, panel_cot, inverses):
    width = inverses.shape[-1]
    chips = lax.axis_size("row") // 2
    lane = width // 4
    f32, dma = jnp.float32, pltpu.SemaphoreType.DMA
    anywhere = pl.BlockSpec(memory_space=pl.ANY)

    def kernel(*refs):
        ring_kernel(chips, *refs)

    adjoint, diag_terms = pl.pallas_call(
        kernel,
        out_shape=(
            jax.ShapeDtypeStruct(panels.shape, f32),
            jax.ShapeDtypeStruct(inverses.shape, f32),
        ),
        in_specs=[anywhere] * 4,
        out_specs=(anywhere, anywhere),
        scratch_shapes=[
            pltpu.VMEM((chips, width, width), f32),
            pltpu.VMEM(panels.shape, f32),
            pltpu.VMEM(panels.shape, f32),
            pltpu.VMEM(inverses.shape, f32),
            pltpu.VMEM((2 * width, width), jnp.bfloat16),
            pltpu.VMEM((2 * width, width), jnp.bfloat16),
            pltpu.VMEM((2, 2, chips, 2, lane, width), f32),
            pltpu.VMEM((2, 2, chips, lane, width), f32),
            pltpu.VMEM((2, 2, chips - 1, lane, width), f32),
            pltpu.VMEM((2, 2, 2, lane, width), f32),
            pltpu.VMEM(panels.shape, f32),
            pltpu.VMEM(inverses.shape, f32),
            dma((chips + 3,)),
            dma((2, 2)),
            dma((2, 2, chips)),
            dma((2, 2, chips)),
            dma((2, 2, chips - 1, SUBS)),
            dma((2, 2, chips - 1, SUBS)),
            dma((2, 2, 2)),
            dma((2, 2, 2)),
        ],
        compiler_params=pltpu.CompilerParams(
            collective_id=0, has_side_effects=True, vmem_limit_bytes=62 * 1024 * 1024
        ),
    )(gbar, panels, panel_cot, inverses)
    diag_adjoint = lax.psum_scatter(diag_terms, "row", scatter_dimension=1, tiled=True)
    return adjoint, diag_adjoint


def plain_device(gbar, panels, panel_cot, inverses):
    width = inverses.shape[-1]
    mode = lax.Precision.HIGHEST
    row_id = lax.axis_index("row")
    col_count = lax.axis_size("col")
    contract = (((0,), (0,)), ((), ()))
    partial_value = lax.dot_general(
        gbar, panels, contract, precision=mode, preferred_element_type=jnp.float32
    )
    summed = lax.psum(partial_value, "row")
    own_tile = lax.dynamic_slice_in_dim(summed, row_id // col_count * width, width, 0)
    own_tile = jnp.where(lax.axis_index("col") == row_id % col_count, own_tile, 0)
    combined = panel_cot - 2.0 * lax.psum(own_tile, "col")
    adjoint, terms = [], []
    for panel in (0, 1):
        columns = slice(panel * width, (panel + 1) * width)
        adjoint.append(
            jnp.dot(combined[:, columns], inverses[panel], precision=mode, preferred_element_type=jnp.float32)
        )
        terms.append(
            -lax.dot_general(
                adjoint[-1], panels[:, columns], contract, precision=mode, preferred_element_type=jnp.float32
            )
        )
    diag_adjoint = lax.psum_scatter(jnp.stack(terms), "row", scatter_dimension=1, tiled=True)
    return jnp.concatenate(adjoint, axis=1), diag_adjoint


def solution(mesh):
    in_specs = (P("row", "col"), P("row", None), P("row", None), P())
    out_specs = (P("row", None), P(None, "row", None))
    on_ring = mesh.shape["col"] == 2 and mesh.shape["row"] == 16
    return jax.shard_map(
        ring_device if on_ring else plain_device,
        mesh=mesh, in_specs=in_specs, out_specs=out_specs, check_vma=False,
    )
```

```python
import jax
import jax.numpy as jnp
from jax import lax
from jax.experimental import pallas as pl
from jax.experimental.pallas import tpu as pltpu
from jax.sharding import PartitionSpec as P

MESH = pl.DeviceIdType.MESH
SUBS = 2


def halves(value):
    high = value.astype(jnp.bfloat16)
    low = (value - high.astype(jnp.float32)).astype(jnp.bfloat16)
    return high, low


def product(left, right):
    (left_high, left_low), (right_high, right_low) = left, right

    def one(a, b):
        return jnp.dot(a, b, preferred_element_type=jnp.float32)

    return one(left_high, right_low) + one(left_low, right_high) + one(left_high, right_high)


def ring_kernel(
    chips, gbar, panels, cot, inverses,
    adjoint, diag,
    g_v, p_v, cot_t, inv_v, inv_high, inv_low, p_high, p_low, terms, other, arrived, final, adj_v,
    diag_v, diag_mate, diag_parts, diag_out,
    load_sems, out_sems, pair_send, pair_recv, ring_send, ring_recv, end_send, end_recv,
    mate_sems, part_send, part_recv, swap_sems,
):
    width = inverses.shape[-1]
    lane = width // 4
    piece = lane // SUBS
    row = lax.axis_index("row")
    col = lax.axis_index("col")
    chip = row // 2
    core = row % 2
    mate = 1 - core
    half = chips // 2

    def place_of(chip_id):
        return jnp.where(chip_id % 2 == 0, chip_id // 2, chips - 1 - chip_id // 2)

    def chip_at(place):
        return jnp.where(place < half, 2 * place, 2 * (chips - 1 - place) + 1)

    place = place_of(chip)
    right = chip_at((place + 1) % chips)
    left = chip_at((place + chips - 1) % chips)

    def tile_at(way, step):
        ahead = jnp.where(way == 0, place + 2 * chips - 1 - step, place + 1 + step)
        return chip_at(ahead % chips)

    def load_g(tile):
        start = pl.multiple_of(tile * width, width)
        return pltpu.make_async_copy(gbar.at[:, pl.ds(start, width)], g_v.at[tile], load_sems.at[tile])

    def load_p(panel):
        columns = slice(panel * width, (panel + 1) * width)
        return pltpu.make_async_copy(
            panels.at[:, columns], p_v.at[:, columns], load_sems.at[chips + panel]
        )

    load_cot = pltpu.make_async_copy(cot, adj_v, load_sems.at[chips + 2])
    load_inv = pltpu.make_async_copy(inverses, inv_v, load_sems.at[chips + 3])
    load_p(0).start()
    for hop in (1, 2, 3):
        load_g(chip_at((place + chips - hop) % chips)).start()
        load_g(chip_at((place + hop) % chips)).start()
    load_g(chip_at((place + half) % chips)).start()
    load_g(chip).start()
    load_p(1).start()
    load_cot.start()
    load_inv.start()

    barrier = pltpu.get_barrier_semaphore()
    friends = [(2 * ((chip + hop) % chips) + core, col) for hop in range(1, chips)] + [
        (2 * chip + mate, col),
        (2 * chip + core, 1 - col),
        (2 * chip + mate, 1 - col),
    ]
    for friend in friends:
        pl.semaphore_signal(barrier, inc=1, device_id=friend, device_id_type=MESH)

    def turn_p(panel):
        load_p(panel).wait()
        for block in (2 * panel, 2 * panel + 1):
            rows = slice(block * width // 2, (block + 1) * width // 2)
            high, low = halves(p_v[:, rows].T)
            p_high[rows, :] = high
            p_low[rows, :] = low

    def turn_rest():
        load_cot.wait()
        load_inv.wait()
        for panel in (0, 1):
            cot_t[panel] = adj_v[:, panel * width:(panel + 1) * width].T
            high, low = halves(inv_v[panel].T)
            inv_high[panel] = high
            inv_low[panel] = low

    turn_p(0)

    def pair_copy(panel, way, step):
        return pltpu.make_async_remote_copy(
            terms.at[panel, way, step, mate],
            other.at[panel, way, step],
            pair_send.at[panel, way, step],
            pair_recv.at[panel, way, step],
            device_id=(2 * chip + mate, col),
            device_id_type=MESH,
        )

    def ring_copy(panel, way, step, sub):
        target = jnp.where(way == 0, right, left)
        rows = pl.ds(sub * piece, piece)
        return pltpu.make_async_remote_copy(
            terms.at[panel, way, step, core, rows],
            arrived.at[panel, way, step, rows],
            ring_send.at[panel, way, step, sub],
            ring_recv.at[panel, way, step, sub],
            device_id=(2 * target + core, col),
            device_id_type=MESH,
        )

    def end_copy(panel, way, plane, source_core, sub):
        rows = pl.ds(sub * piece, piece)
        return pltpu.make_async_remote_copy(
            terms.at[panel, way, chips - 1, source_core, rows],
            final.at[panel, way, source_core, rows],
            end_send.at[panel, way, plane, sub],
            end_recv.at[panel, way, source_core, sub],
            device_id=(2 * chip + col, col if plane == 0 else 1 - col),
            device_id_type=MESH,
        )

    def end_local(panel, way, source_core, sub):
        rows = pl.ds(sub * piece, piece)
        return pltpu.make_async_copy(
            terms.at[panel, way, chips - 1, source_core, rows],
            final.at[panel, way, source_core, rows],
            end_recv.at[panel, way, source_core, sub],
        )

    def make_terms(count):
        panel, step = count // chips, count % chips
        for way in (0, 1):
            tile = tile_at(way, step)

            @pl.when((panel == 0) & (step < half if way == 0 else step < half - 1))
            def _():
                load_g(tile).wait()

            @pl.when((panel == 0) & (step == chips - 1) & (way == 0))
            def _():
                load_g(tile).wait()

            rows = pl.ds(pl.multiple_of(panel * width + way * (width // 2), width // 2), width // 2)
            value = product((p_high[rows, :], p_low[rows, :]), halves(g_v[tile]))
            terms[panel, way, step, 0] = value[:lane]
            terms[panel, way, step, 1] = value[lane:]
            pair_copy(panel, way, step).start()

    def ring_step(count):
        panel, step = count // chips, count % chips
        for way in (0, 1):
            pair_copy(panel, way, step).wait_recv()
        for sub in range(SUBS):
            rows = pl.ds(sub * piece, piece)
            for way in (0, 1):
                @pl.when(step > 0)
                def _():
                    ring_copy(panel, way, step - 1, sub).wait_recv()
                    terms[panel, way, step, core, rows] = (
                        terms[panel, way, step, core, rows]
                        + other[panel, way, step, rows]
                        + arrived[panel, way, step - 1, rows]
                    )

                @pl.when(step == 0)
                def _():
                    terms[panel, way, step, core, rows] = (
                        terms[panel, way, step, core, rows] + other[panel, way, step, rows]
                    )

                @pl.when(step < chips - 1)
                def _():
                    ring_copy(panel, way, step, sub).start()

                @pl.when(step == chips - 1)
                def _():
                    end_copy(panel, way, 1, core, sub).start()

                @pl.when((step == chips - 1) & (core == col))
                def _():
                    end_local(panel, way, core, sub).start()

                @pl.when((step == chips - 1) & (core != col))
                def _():
                    end_copy(panel, way, 0, core, sub).start()

    side = pl.ds(pl.multiple_of(col * (width // 2), width // 2), width // 2)
    short = width // (2 * chips)

    def mate_copy(panel):
        return pltpu.make_async_remote_copy(
            diag_v.at[panel, :, mate],
            diag_mate.at[panel],
            mate_sems.at[0, panel],
            mate_sems.at[1, panel],
            device_id=(2 * chip + mate, col),
            device_id_type=MESH,
        )

    def part_copy(panel, source, target):
        return pltpu.make_async_remote_copy(
            diag_v.at[panel, target, core],
            diag_parts.at[panel, source],
            part_send.at[panel, target],
            part_recv.at[panel, source],
            device_id=(2 * target + core, col),
            device_id_type=MESH,
        )

    def swap_copy(panel):
        return pltpu.make_async_remote_copy(
            diag_out.at[panel, :, side],
            diag_out.at[panel, :, side],
            swap_sems.at[0, panel],
            swap_sems.at[1, panel],
            device_id=(2 * chip + core, 1 - col),
            device_id_type=MESH,
        )

    def adjoint_out(panel):
        columns = slice(panel * width, (panel + 1) * width)
        return pltpu.make_async_copy(adj_v.at[:, columns], adjoint.at[:, columns], out_sems.at[panel])

    def finish(panel):
        for way in (0, 1):
            for source in (0, 1):
                for sub in range(SUBS):
                    end_local(panel, way, source, sub).wait()
        combined = cot_t[panel] - 2.0 * final[panel].reshape(width, width)
        turned = product((inv_high[panel], inv_low[panel]), halves(combined))
        start = pl.multiple_of(panel * width + col * (width // 2), width // 2)
        own = p_v[:, pl.ds(start, width // 2)]
        diag_v[panel] = -product(halves(turned), halves(own)).reshape(chips, 2, short, width // 2)
        mate_copy(panel).start()
        adj_v[:, panel * width:(panel + 1) * width] = turned.T
        adjoint_out(panel).start()

    def scatter(panel):
        mate_copy(panel).wait_recv()
        diag_v[panel, :, core] = diag_v[panel, :, core] + diag_mate[panel]
        for hop in range(1, chips):
            part_copy(panel, chip, (chip + hop) % chips).start()

    def collect(panel):
        total = diag_v[panel, chip, core]
        for hop in range(1, chips):
            source = (chip + hop) % chips
            part_copy(panel, source, chip).wait_recv()
            total = total + diag_parts[panel, source]
        diag_out[panel, :, side] = total
        swap_copy(panel).start()

    pl.semaphore_wait(barrier, len(friends))
    make_terms(jnp.int32(0))

    def body(count, carry):
        @pl.when(count < 2 * chips - 1)
        def _():
            make_terms(count + 1)

        ring_step(count)

        @pl.when(count == 2)
        def _():
            turn_p(1)
            turn_rest()

        @pl.when(count == chips + 2)
        def _():
            finish(0)

        @pl.when(count == chips + 3)
        def _():
            scatter(0)

        @pl.when(count == chips + 5)
        def _():
            collect(0)

        return carry

    lax.fori_loop(0, 2 * chips, body, 0)
    finish(1)
    scatter(1)
    collect(1)

    def drain(count, carry):
        panel, step = count // chips, count % chips
        for way in (0, 1):
            pair_copy(panel, way, step).wait_send()

            @pl.when(step < chips - 1)
            def _():
                for sub in range(SUBS):
                    ring_copy(panel, way, step, sub).wait_send()

        return carry

    lax.fori_loop(0, 2 * chips, drain, 0)
    for panel in (0, 1):
        for way in (0, 1):
            for sub in range(SUBS):
                end_copy(panel, way, 1, core, sub).wait_send()

                @pl.when(core != col)
                def _():
                    end_copy(panel, way, 0, core, sub).wait_send()

        mate_copy(panel).wait_send()
        for hop in range(1, chips):
            part_copy(panel, chip, (chip + hop) % chips).wait_send()
        swap_copy(panel).wait()
        adjoint_out(panel).wait()
    store = pltpu.make_async_copy(diag_out, diag, out_sems.at[2])
    store.start()
    store.wait()


def ring_device(gbar, panels, panel_cot, inverses):
    width = inverses.shape[-1]
    chips = lax.axis_size("row") // 2
    lane = width // 4
    f32, dma = jnp.float32, pltpu.SemaphoreType.DMA
    anywhere = pl.BlockSpec(memory_space=pl.ANY)

    def kernel(*refs):
        ring_kernel(chips, *refs)

    short = width // (2 * chips)
    bf16 = jnp.bfloat16
    return pl.pallas_call(
        kernel,
        out_shape=(
            jax.ShapeDtypeStruct(panels.shape, f32),
            jax.ShapeDtypeStruct((2, short, width), f32),
        ),
        in_specs=[anywhere] * 4,
        out_specs=(anywhere, anywhere),
        scratch_shapes=[
            pltpu.VMEM((chips, width, width), f32),
            pltpu.VMEM(panels.shape, f32),
            pltpu.VMEM(inverses.shape, f32),
            pltpu.VMEM(inverses.shape, f32),
            pltpu.VMEM(inverses.shape, bf16),
            pltpu.VMEM(inverses.shape, bf16),
            pltpu.VMEM((2 * width, width), bf16),
            pltpu.VMEM((2 * width, width), bf16),
            pltpu.VMEM((2, 2, chips, 2, lane, width), f32),
            pltpu.VMEM((2, 2, chips, lane, width), f32),
            pltpu.VMEM((2, 2, chips - 1, lane, width), f32),
            pltpu.VMEM((2, 2, 2, lane, width), f32),
            pltpu.VMEM(panels.shape, f32),
            pltpu.VMEM((2, chips, 2, short, width // 2), f32),
            pltpu.VMEM((2, chips, short, width // 2), f32),
            pltpu.VMEM((2, chips, short, width // 2), f32),
            pltpu.VMEM((2, short, width), f32),
            dma((chips + 4,)),
            dma((3,)),
            dma((2, 2, chips)),
            dma((2, 2, chips)),
            dma((2, 2, chips - 1, SUBS)),
            dma((2, 2, chips - 1, SUBS)),
            dma((2, 2, 2, SUBS)),
            dma((2, 2, 2, SUBS)),
            dma((2, 2)),
            dma((2, chips)),
            dma((2, chips)),
            dma((2, 2)),
        ],
        compiler_params=pltpu.CompilerParams(
            collective_id=0, has_side_effects=True, vmem_limit_bytes=62 * 1024 * 1024
        ),
    )(gbar, panels, panel_cot, inverses)


def plain_device(gbar, panels, panel_cot, inverses):
    width = inverses.shape[-1]
    mode = lax.Precision.HIGHEST
    row_id = lax.axis_index("row")
    col_count = lax.axis_size("col")
    contract = (((0,), (0,)), ((), ()))
    partial_value = lax.dot_general(
        gbar, panels, contract, precision=mode, preferred_element_type=jnp.float32
    )
    summed = lax.psum(partial_value, "row")
    own_tile = lax.dynamic_slice_in_dim(summed, row_id // col_count * width, width, 0)
    own_tile = jnp.where(lax.axis_index("col") == row_id % col_count, own_tile, 0)
    combined = panel_cot - 2.0 * lax.psum(own_tile, "col")
    adjoint, terms = [], []
    for panel in (0, 1):
        columns = slice(panel * width, (panel + 1) * width)
        adjoint.append(
            jnp.dot(combined[:, columns], inverses[panel], precision=mode, preferred_element_type=jnp.float32)
        )
        terms.append(
            -lax.dot_general(
                adjoint[-1], panels[:, columns], contract, precision=mode, preferred_element_type=jnp.float32
            )
        )
    diag_adjoint = lax.psum_scatter(jnp.stack(terms), "row", scatter_dimension=1, tiled=True)
    return jnp.concatenate(adjoint, axis=1), diag_adjoint


def solution(mesh):
    in_specs = (P("row", "col"), P("row", None), P("row", None), P())
    out_specs = (P("row", None), P(None, "row", None))
    on_ring = mesh.shape["col"] == 2 and mesh.shape["row"] == 16
    return jax.shard_map(
        ring_device if on_ring else plain_device,
        mesh=mesh, in_specs=in_specs, out_specs=out_specs, check_vma=False,
    )
```

```python
import jax
import jax.numpy as jnp
from jax import lax
from jax.experimental import pallas as pl
from jax.experimental.pallas import tpu as pltpu
from jax.sharding import PartitionSpec as P

MESH = pl.DeviceIdType.MESH
SUBS = 4
PARTS = 2


def halves(value):
    high = value.astype(jnp.bfloat16)
    low = (value - high.astype(jnp.float32)).astype(jnp.bfloat16)
    return high, low


def product(left, right):
    (left_high, left_low), (right_high, right_low) = left, right

    def one(a, b):
        return jnp.dot(a, b, preferred_element_type=jnp.float32)

    return one(left_high, right_low) + one(left_low, right_high) + one(left_high, right_high)


def ring_kernel(
    chips, gbar, panels, cot, inverses,
    adjoint, diag,
    g_v, p_v, cot_t, inv_v, inv_high, inv_low, p_high, p_low, terms, other, arrived, final, adj_v,
    diag_v, diag_mate, diag_parts, diag_out,
    load_sems, out_sems, pair_send, pair_recv, ring_send, ring_recv, end_send, end_recv,
    mate_sems, part_send, part_recv, swap_sems,
):
    width = inverses.shape[-1]
    lane = width // (2 * PARTS)
    piece = lane // SUBS
    total_steps = PARTS * chips
    block = 2 * width // PARTS
    row = lax.axis_index("row")
    col = lax.axis_index("col")
    chip = row // 2
    core = row % 2
    mate = 1 - core
    half = chips // 2

    def place_of(chip_id):
        return jnp.where(chip_id % 2 == 0, chip_id // 2, chips - 1 - chip_id // 2)

    def chip_at(place):
        return jnp.where(place < half, 2 * place, 2 * (chips - 1 - place) + 1)

    place = place_of(chip)
    right = chip_at((place + 1) % chips)
    left = chip_at((place + chips - 1) % chips)

    def tile_at(way, step):
        ahead = jnp.where(way == 0, place + 2 * chips - 1 - step, place + 1 + step)
        return chip_at(ahead % chips)

    def load_g(tile):
        start = pl.multiple_of(tile * width, width)
        return pltpu.make_async_copy(gbar.at[:, pl.ds(start, width)], g_v.at[tile], load_sems.at[tile])

    def load_p(panel):
        columns = slice(panel * width, (panel + 1) * width)
        return pltpu.make_async_copy(
            panels.at[:, columns], p_v.at[:, columns], load_sems.at[chips + panel]
        )

    load_cot = pltpu.make_async_copy(cot, adj_v, load_sems.at[chips + 2])
    load_inv = pltpu.make_async_copy(inverses, inv_v, load_sems.at[chips + 3])
    load_p(0).start()
    for hop in (1, 2, 3):
        load_g(chip_at((place + chips - hop) % chips)).start()
        load_g(chip_at((place + hop) % chips)).start()
    load_g(chip_at((place + half) % chips)).start()
    load_g(chip).start()
    load_p(1).start()
    load_cot.start()
    load_inv.start()

    barrier = pltpu.get_barrier_semaphore()
    friends = [(2 * ((chip + hop) % chips) + core, col) for hop in range(1, chips)] + [
        (2 * chip + mate, col),
        (2 * chip + core, 1 - col),
        (2 * chip + mate, 1 - col),
    ]
    for friend in friends:
        pl.semaphore_signal(barrier, inc=1, device_id=friend, device_id_type=MESH)

    def turn_p(part):
        if part % (PARTS // 2) == 0:
            load_p(part // (PARTS // 2)).wait()
        rows = slice(part * block, (part + 1) * block)
        high, low = halves(p_v[:, rows].T)
        p_high[rows, :] = high
        p_low[rows, :] = low

    def turn_cot(panel):
        if panel == 0:
            load_cot.wait()
        cot_t[panel] = adj_v[:, panel * width:(panel + 1) * width].T

    def turn_inv(panel):
        if panel == 0:
            load_inv.wait()
        high, low = halves(inv_v[panel].T)
        inv_high[panel] = high
        inv_low[panel] = low

    turn_p(0)

    def pair_copy(panel, way, step):
        return pltpu.make_async_remote_copy(
            terms.at[panel, way, step, mate],
            other.at[panel, way, step],
            pair_send.at[panel, way, step],
            pair_recv.at[panel, way, step],
            device_id=(2 * chip + mate, col),
            device_id_type=MESH,
        )

    def ring_copy(panel, way, step, sub):
        target = jnp.where(way == 0, right, left)
        rows = pl.ds(sub * piece, piece)
        return pltpu.make_async_remote_copy(
            terms.at[panel, way, step, core, rows],
            arrived.at[panel, way, step, rows],
            ring_send.at[panel, way, step, sub],
            ring_recv.at[panel, way, step, sub],
            device_id=(2 * target + core, col),
            device_id_type=MESH,
        )

    def end_copy(panel, way, plane, source_core, sub):
        rows = pl.ds(sub * piece, piece)
        return pltpu.make_async_remote_copy(
            terms.at[panel, way, chips - 1, source_core, rows],
            final.at[panel, way, source_core, rows],
            end_send.at[panel, way, plane, sub],
            end_recv.at[panel, way, source_core, sub],
            device_id=(2 * chip + col, col if plane == 0 else 1 - col),
            device_id_type=MESH,
        )

    def end_local(panel, way, source_core, sub):
        rows = pl.ds(sub * piece, piece)
        return pltpu.make_async_copy(
            terms.at[panel, way, chips - 1, source_core, rows],
            final.at[panel, way, source_core, rows],
            end_recv.at[panel, way, source_core, sub],
        )

    def make_terms(count):
        panel, step = count // chips, count % chips
        for way in (0, 1):
            tile = tile_at(way, step)

            @pl.when((panel == 0) & (step < half if way == 0 else step < half - 1))
            def _():
                load_g(tile).wait()

            @pl.when((panel == 0) & (step == chips - 1) & (way == 0))
            def _():
                load_g(tile).wait()

            rows = pl.ds(pl.multiple_of(panel * block + way * (block // 2), block // 2), block // 2)
            value = product((p_high[rows, :], p_low[rows, :]), halves(g_v[tile]))
            terms[panel, way, step, 0] = value[:lane]
            terms[panel, way, step, 1] = value[lane:]
            pair_copy(panel, way, step).start()

    def ring_step(count):
        panel, step = count // chips, count % chips
        for way in (0, 1):
            pair_copy(panel, way, step).wait_recv()
        for sub in range(SUBS):
            rows = pl.ds(sub * piece, piece)
            for way in (0, 1):
                @pl.when(step > 0)
                def _():
                    ring_copy(panel, way, step - 1, sub).wait_recv()
                    terms[panel, way, step, core, rows] = (
                        terms[panel, way, step, core, rows]
                        + other[panel, way, step, rows]
                        + arrived[panel, way, step - 1, rows]
                    )

                @pl.when(step == 0)
                def _():
                    terms[panel, way, step, core, rows] = (
                        terms[panel, way, step, core, rows] + other[panel, way, step, rows]
                    )

                @pl.when(step < chips - 1)
                def _():
                    ring_copy(panel, way, step, sub).start()

                @pl.when(step == chips - 1)
                def _():
                    end_copy(panel, way, 1, core, sub).start()

                @pl.when((step == chips - 1) & (core == col))
                def _():
                    end_local(panel, way, core, sub).start()

                @pl.when((step == chips - 1) & (core != col))
                def _():
                    end_copy(panel, way, 0, core, sub).start()

    side = pl.ds(pl.multiple_of(col * (width // 2), width // 2), width // 2)
    short = width // (2 * chips)

    def mate_copy(panel):
        return pltpu.make_async_remote_copy(
            diag_v.at[panel, :, mate],
            diag_mate.at[panel],
            mate_sems.at[0, panel],
            mate_sems.at[1, panel],
            device_id=(2 * chip + mate, col),
            device_id_type=MESH,
        )

    def part_copy(panel, source, target):
        return pltpu.make_async_remote_copy(
            diag_v.at[panel, target, core],
            diag_parts.at[panel, source],
            part_send.at[panel, target],
            part_recv.at[panel, source],
            device_id=(2 * target + core, col),
            device_id_type=MESH,
        )

    def swap_copy(panel):
        return pltpu.make_async_remote_copy(
            diag_out.at[panel, :, side],
            diag_out.at[panel, :, side],
            swap_sems.at[0, panel],
            swap_sems.at[1, panel],
            device_id=(2 * chip + core, 1 - col),
            device_id_type=MESH,
        )

    def adjoint_out(panel):
        columns = slice(panel * width, (panel + 1) * width)
        return pltpu.make_async_copy(adj_v.at[:, columns], adjoint.at[:, columns], out_sems.at[panel])

    def solve(panel):
        for part in range(panel * PARTS // 2, (panel + 1) * PARTS // 2):
            for way in (0, 1):
                for source in (0, 1):
                    for sub in range(SUBS):
                        end_local(part, way, source, sub).wait()
        coupled = final[panel * PARTS // 2:(panel + 1) * PARTS // 2].reshape(width, width)
        turned = product((inv_high[panel], inv_low[panel]), halves(cot_t[panel] - 2.0 * coupled))
        cot_t[panel] = turned

    def diagonal(panel):
        start = pl.multiple_of(panel * width + col * (width // 2), width // 2)
        own = p_v[:, pl.ds(start, width // 2)]
        value = -product(halves(cot_t[panel]), halves(own))
        diag_v[panel] = value.reshape(chips, 2, short, width // 2)
        mate_copy(panel).start()

    def give(panel):
        adj_v[:, panel * width:(panel + 1) * width] = cot_t[panel].T
        adjoint_out(panel).start()

    def scatter(panel):
        mate_copy(panel).wait_recv()
        diag_v[panel, :, core] = diag_v[panel, :, core] + diag_mate[panel]
        for hop in range(1, chips):
            part_copy(panel, chip, (chip + hop) % chips).start()

    def collect(panel):
        total = diag_v[panel, chip, core]
        for hop in range(1, chips):
            source = (chip + hop) % chips
            part_copy(panel, source, chip).wait_recv()
            total = total + diag_parts[panel, source]
        diag_out[panel, :, side] = total
        swap_copy(panel).start()

    pl.semaphore_wait(barrier, len(friends))
    make_terms(jnp.int32(0))
    ring_step(jnp.int32(0))
    make_terms(jnp.int32(1))
    make_terms(jnp.int32(2))
    second = total_steps // 2
    chores = {
        1: lambda: turn_p(1),
        2: lambda: turn_cot(0),
        3: lambda: turn_cot(1),
        4: lambda: turn_inv(0),
        5: lambda: turn_inv(1),
        second + 2: lambda: solve(0),
        second + 3: lambda: diagonal(0),
        second + 5: lambda: give(0),
        second + 4: lambda: scatter(0),
        second + 6: lambda: collect(0),
    }

    def body(count, carry):
        @pl.when(count < total_steps - 2)
        def _():
            make_terms(count + 2)

        step = count % chips
        early = (step == chips - 1) & (count < total_steps - 1)
        ring_step(jnp.where(early, count + 1, jnp.where(step == 0, count - 1, count)))
        for at, chore in chores.items():
            pl.when(count == at)(chore)
        return carry

    lax.fori_loop(1, total_steps, body, 0)
    solve(1)
    diagonal(1)
    scatter(1)
    give(1)
    collect(1)

    def drain(count, carry):
        panel, step = count // chips, count % chips
        for way in (0, 1):
            pair_copy(panel, way, step).wait_send()

            @pl.when(step < chips - 1)
            def _():
                for sub in range(SUBS):
                    ring_copy(panel, way, step, sub).wait_send()

        return carry

    lax.fori_loop(0, total_steps, drain, 0)
    for part in range(PARTS):
        for way in (0, 1):
            for sub in range(SUBS):
                end_copy(part, way, 1, core, sub).wait_send()

                @pl.when(core != col)
                def _():
                    end_copy(part, way, 0, core, sub).wait_send()

    for panel in (0, 1):
        mate_copy(panel).wait_send()
        for hop in range(1, chips):
            part_copy(panel, chip, (chip + hop) % chips).wait_send()
        swap_copy(panel).wait()
        adjoint_out(panel).wait()
    store = pltpu.make_async_copy(diag_out, diag, out_sems.at[2])
    store.start()
    store.wait()


def ring_device(gbar, panels, panel_cot, inverses):
    width = inverses.shape[-1]
    chips = lax.axis_size("row") // 2
    lane = width // (2 * PARTS)
    f32, dma = jnp.float32, pltpu.SemaphoreType.DMA
    anywhere = pl.BlockSpec(memory_space=pl.ANY)

    def kernel(*refs):
        ring_kernel(chips, *refs)

    short = width // (2 * chips)
    bf16 = jnp.bfloat16
    return pl.pallas_call(
        kernel,
        out_shape=(
            jax.ShapeDtypeStruct(panels.shape, f32),
            jax.ShapeDtypeStruct((2, short, width), f32),
        ),
        in_specs=[anywhere] * 4,
        out_specs=(anywhere, anywhere),
        scratch_shapes=[
            pltpu.VMEM((chips, width, width), f32),
            pltpu.VMEM(panels.shape, f32),
            pltpu.VMEM(inverses.shape, f32),
            pltpu.VMEM(inverses.shape, f32),
            pltpu.VMEM(inverses.shape, bf16),
            pltpu.VMEM(inverses.shape, bf16),
            pltpu.VMEM((2 * width, width), bf16),
            pltpu.VMEM((2 * width, width), bf16),
            pltpu.VMEM((PARTS, 2, chips, 2, lane, width), f32),
            pltpu.VMEM((PARTS, 2, chips, lane, width), f32),
            pltpu.VMEM((PARTS, 2, chips - 1, lane, width), f32),
            pltpu.VMEM((PARTS, 2, 2, lane, width), f32),
            pltpu.VMEM(panels.shape, f32),
            pltpu.VMEM((2, chips, 2, short, width // 2), f32),
            pltpu.VMEM((2, chips, short, width // 2), f32),
            pltpu.VMEM((2, chips, short, width // 2), f32),
            pltpu.VMEM((2, short, width), f32),
            dma((chips + 4,)),
            dma((3,)),
            dma((PARTS, 2, chips)),
            dma((PARTS, 2, chips)),
            dma((PARTS, 2, chips - 1, SUBS)),
            dma((PARTS, 2, chips - 1, SUBS)),
            dma((PARTS, 2, 2, SUBS)),
            dma((PARTS, 2, 2, SUBS)),
            dma((2, 2)),
            dma((2, chips)),
            dma((2, chips)),
            dma((2, 2)),
        ],
        compiler_params=pltpu.CompilerParams(
            collective_id=0, has_side_effects=True, vmem_limit_bytes=62 * 1024 * 1024
        ),
    )(gbar, panels, panel_cot, inverses)


def plain_device(gbar, panels, panel_cot, inverses):
    width = inverses.shape[-1]
    mode = lax.Precision.HIGHEST
    row_id = lax.axis_index("row")
    col_count = lax.axis_size("col")
    contract = (((0,), (0,)), ((), ()))
    partial_value = lax.dot_general(
        gbar, panels, contract, precision=mode, preferred_element_type=jnp.float32
    )
    summed = lax.psum(partial_value, "row")
    own_tile = lax.dynamic_slice_in_dim(summed, row_id // col_count * width, width, 0)
    own_tile = jnp.where(lax.axis_index("col") == row_id % col_count, own_tile, 0)
    combined = panel_cot - 2.0 * lax.psum(own_tile, "col")
    adjoint, terms = [], []
    for panel in (0, 1):
        columns = slice(panel * width, (panel + 1) * width)
        adjoint.append(
            jnp.dot(combined[:, columns], inverses[panel], precision=mode, preferred_element_type=jnp.float32)
        )
        terms.append(
            -lax.dot_general(
                adjoint[-1], panels[:, columns], contract, precision=mode, preferred_element_type=jnp.float32
            )
        )
    diag_adjoint = lax.psum_scatter(jnp.stack(terms), "row", scatter_dimension=1, tiled=True)
    return jnp.concatenate(adjoint, axis=1), diag_adjoint


def solution(mesh):
    in_specs = (P("row", "col"), P("row", None), P("row", None), P())
    out_specs = (P("row", None), P(None, "row", None))
    on_ring = mesh.shape["col"] == 2 and mesh.shape["row"] == 16
    return jax.shard_map(
        ring_device if on_ring else plain_device,
        mesh=mesh, in_specs=in_specs, out_specs=out_specs, check_vma=False,
    )
```
